32 devices in a mesh: groups: 2 (over x), tensor: 16 (over z, y, core).
Axes of the slice: x: 2, y: 2, z: 4, core: 2. Of those that a mesh axis runs over, the one named last changes fastest.
Arguments:
- hidden_in: bfloat16 [4, 32, 12288], P(None, ('groups', 'tensor')), parts along dimension 1, may hold values from -6 to 6
- active: int32 [4, 32, 4], P(None, ('groups', 'tensor')), parts along dimension 1, may hold values from 0 to 31, as said below
- ln_gain: float32 [12288], replicated, may hold values from 0.1 to 1.9
- ln_bias: float32 [12288], replicated, may hold values from -2 to 2
- up_weight: bfloat16 [12288, 4096], P(None, 'tensor'), may hold values from -0.0546875 to 0.0546875
- up_bias: float32 [4096], P('tensor'), may hold values from -3 to 3
- down_weight: bfloat16 [4096, 12288], P('tensor'), may hold values from -0.25 to 0.25
- down_bias: float32 [12288], replicated, may hold values from -3 to 3
Outputs:
- mixed: bfloat16 [4, 32, 12288], P(None, ('groups', 'tensor')), parts along dimension 1
The draws below stay inside these ranges and needn't reach their ends.
There are 2 independent parts, one for each index of `groups`. The reference program is written for one: setup_inputs(seed, part) draws one part's arguments, and reference() takes and returns one part's arrays. A program takes and returns all parts, laid end to end along the dimension named above; an argument that names none is the same for every part. Nothing has to cross between parts.
Inputs may be any that keep to these rules, and one draw needn't show every extreme that they name: `active`: the 4 block ids of a row are distinct. Among the 4 rows that one index of tensor holds, at most 2 name blocks of any one index of tensor (block id // 2), and some index of tensor is named by exactly 2 of them in every draw.
All inputs are finite; a program needn't handle non-finite values.
Results may differ from the reference program's by a relative error of at most 0.0045.
Values may be sent and summed in bfloat16 or wider, within the bound.
A program may use at most 128 MiB of HBM per device.

```python
import jax
import jax.numpy as jnp
from jax import lax

D = 12288
BLOCK = 128
BLOCKS_DEV = 2
STEPS = 4
ROWS_DEV = 1
ROWS = 16
BLOCKS = 32
FF = 4096
ACTIVE = 4


def draw_active(key, part):
    key = jax.random.fold_in(key, 7)
    devices = ROWS // ROWS_DEV
    row_steps = STEPS * ROWS_DEV
    key_perm, key_hot, key_warm, key_noise = jax.random.split(key, 4)
    orders = jax.vmap(lambda k: jax.random.permutation(k, devices))(jax.random.split(key_perm, devices))
    offsets = (orders % row_steps).astype(jnp.int32)
    positions = jnp.arange(row_steps, dtype=jnp.int32)
    allowed = (positions[None, :, None] - offsets[:, None, :]) % row_steps < row_steps // 2
    allowed = jnp.repeat(allowed, BLOCKS_DEV, axis=2).astype(jnp.int32)
    block_ids = jnp.arange(BLOCKS, dtype=jnp.int32)
    hot_device = jax.random.randint(key_hot, (), 0, devices, dtype=jnp.int32)
    hot = (block_ids // BLOCKS_DEV == hot_device).astype(jnp.int32)
    warm = jax.random.randint(key_warm, (BLOCKS,), 0, 4, dtype=jnp.int32)
    noise = jax.random.randint(key_noise, (devices, row_steps, BLOCKS), 0, 2 ** 15, dtype=jnp.int32)
    score = allowed * 2 ** 27 + hot[None, None, :] * 2 ** 26 + warm[None, None, :] * 2 ** 24 + noise * 2 ** 9 + block_ids[None, None, :]
    picked = lax.top_k(score, ACTIVE)[1].astype(jnp.int32)
    picked = picked.reshape(devices, STEPS, ROWS_DEV, ACTIVE).transpose(1, 0, 2, 3)
    return picked.reshape(STEPS, ROWS, ACTIVE)


def block_levels(own_key, extent, cuts, low, largest):
    loudness = 1.0
    for axis_at, blocks in cuts:
        heights = jax.random.uniform(jax.random.fold_in(jax.random.fold_in(own_key, 6), axis_at), (blocks,), jnp.float32, low / len(cuts), largest / len(cuts))
        loudness = loudness * jnp.repeat(jnp.exp(heights), extent[axis_at] // blocks).reshape((-1,) + (1,) * (len(extent) - 1 - axis_at))
    return loudness


def bell_draw(rng, dims, scale, limit, cuts=(), kind=jnp.bfloat16):
    array = jax.random.normal(rng, dims, jnp.float32) * scale
    if len(cuts) > 0:
        array = block_levels(rng, dims, cuts, -0.22, 0.18) * array
    return jnp.clip(array, min=-limit, max=limit).astype(kind)


def setup_inputs(seed: int = 0, part: int = 0) -> dict:
    key_list = jax.random.split(jax.random.key(seed), 9)
    part_splits = jax.random.split(jax.random.fold_in(key_list[8], part), 9)
    return {
        "hidden_in": bell_draw(part_splits[0], (STEPS, ROWS, D), 1.0, 6.0, ((1, 16),)),
        "active": draw_active(jax.random.fold_in(jax.random.fold_in(key_list[8], part), 71), part),
        "ln_gain": jnp.clip(1.0 + 0.18 * jax.random.normal(key_list[2], (D,), jnp.float32), 0.1, 1.9),
        "ln_bias": bell_draw(key_list[3], (D,), 0.3, 2.0, (), jnp.float32),
        "up_weight": bell_draw(key_list[4], (D, FF), D ** -0.5, 0.0546875, ((1, 16),)),
        "up_bias": bell_draw(key_list[5], (FF,), 0.5, 3.0, ((0, 16),), jnp.float32),
        "down_weight": bell_draw(key_list[6], (FF, D), (ACTIVE * BLOCK) ** -0.5, 0.25, ((0, 16),)),
        "down_bias": bell_draw(key_list[7], (D,), 0.5, 3.0, (), jnp.float32),
    }


def layer_norm(inputs, gain, shift):
    center = inputs - lax.optimization_barrier(jnp.mean(inputs, axis=-1, keepdims=True))
    spread = lax.optimization_barrier(jnp.mean(center * center, axis=-1, keepdims=True))
    return (center * lax.rsqrt(spread + 1e-05) * gain + shift).astype(jnp.bfloat16)

def reference(hidden_in, active, ln_gain, ln_bias, up_weight, up_bias, down_weight, down_bias):
    shape = hidden_in.shape
    inputs = hidden_in.reshape(-1, D).astype(jnp.float32)
    normed = layer_norm(inputs, ln_gain, ln_bias)
    lists = active.reshape(inputs.shape[0], -1)
    blocks = FF // BLOCK
    live = jnp.any(lists[:, :, None] == jnp.arange(blocks, dtype=jnp.int32)[None, None, :], axis=1)

    def add_block(index, total):
        index = jnp.asarray(index).astype(jnp.int32)
        start = index * BLOCK
        w_up = lax.dynamic_slice_in_dim(up_weight, start, BLOCK, 1)
        bias = lax.dynamic_slice_in_dim(up_bias, start, BLOCK, 0)
        w_down = lax.dynamic_slice_in_dim(down_weight, start, BLOCK, 0)
        keep = lax.dynamic_slice_in_dim(live, index, 1, 1)
        pre = jnp.dot(normed, w_up, preferred_element_type=jnp.float32) + bias
        hidden = jnp.where(keep, jax.nn.relu(pre), 0.0).astype(jnp.bfloat16)
        return total + jnp.dot(hidden, w_down, preferred_element_type=jnp.float32)
    total = lax.fori_loop(0, blocks, add_block, jnp.zeros((inputs.shape[0], D), jnp.float32))
    return (inputs + down_bias + total).astype(jnp.bfloat16).reshape(shape)
```

```python
import functools
import math

import jax
import jax.numpy as jnp
from jax import lax
from jax.experimental import pallas as pl
from jax.experimental.pallas import tpu as pltpu
from jax.sharding import PartitionSpec as P

BLOCK = 128
LANES = 128
PACK = 16
PARTS = 4


def sizes(n_dev):
    cores = 2 if n_dev % 2 == 0 else 1
    rest = n_dev // cores
    mids = math.isqrt(rest)
    while rest % mids:
        mids -= 1
    return rest // mids, mids, cores


def kernel(n_dev, hid, act, gain, shift, up_bias, down_bias, up_hbm, down_hbm, out,
           rows, w_up, w_down, acc, hid_cat, core_in, mid_out, mid_own, mid_in, far_out, far_own, far_in,
           up_sem, down_sem, far_s, far_r, mid_s, mid_r, core_s, core_r,
           rcore_s, rcore_r, rmid_s, rmid_r, rfar_s, rfar_r):
    fars, mids, cores = sizes(n_dev)
    row_count, width = hid.shape
    split = PACK // row_count
    part = width // split
    step = part // PARTS
    units = w_up.shape[2]
    per_dev = units // BLOCK

    me = lax.axis_index("tensor")
    core = lax.rem(me, cores)
    mid = lax.rem(me // cores, mids)
    far = me // (cores * mids)

    def device(c, m, f):
        return {"tensor": (f * mids + m) * cores + c}

    def place(c, m, f):
        return (c * mids + m) * fars + f

    far_peers = [(d, device(core, mid, lax.rem(far + d, fars))) for d in range(1, fars)]
    mid_peers = [(d, device(core, lax.rem(mid + d, mids), far)) for d in range(1, mids)]
    core_peers = [(d, device(lax.rem(core + d, cores), mid, far)) for d in range(1, cores)]
    barrier = pltpu.get_barrier_semaphore()
    for _, peer in far_peers + mid_peers + core_peers:
        pl.semaphore_signal(barrier, inc=1, device_id=peer, device_id_type=pl.DeviceIdType.MESH)

    up_copies, down_copies = [], []
    for c in range(PARTS):
        copy = pltpu.make_async_copy(
            up_hbm.at[:, pl.ds(c * step, step), :], w_up.at[:, pl.ds(c * step, step), :], up_sem.at[c])
        copy.start()
        up_copies.append(copy)

    def remote(src, dst, send, recv, peer):
        copy = pltpu.make_async_remote_copy(
            src_ref=src, dst_ref=dst, send_sem=send, recv_sem=recv,
            device_id=peer, device_id_type=pl.DeviceIdType.MESH)
        copy.start()
        return copy

    x = hid[...].astype(jnp.float32)
    mean = jnp.mean(x, axis=-1, keepdims=True)
    center = x - mean
    scale = lax.rsqrt(jnp.mean(center * center, axis=-1, keepdims=True) + 1e-05)

    mine = place(core, mid, far)
    lane = lax.broadcasted_iota(jnp.int32, (row_count, LANES), 1)
    ids = jnp.full((row_count, LANES), -1, jnp.int32)
    for a in range(act.shape[1]):
        ids = jnp.where(lane == a, act[:, a:a + 1], ids)
    ids = ids.astype(jnp.float32)
    rows[mine, :, 0:LANES] = jnp.concatenate([ids] * split, axis=0).astype(jnp.bfloat16)

    def spans(c):
        start = 0 if c == 0 else LANES + c * step
        return pl.ds(start, step + (LANES if c == 0 else 0))

    def norm_part(c):
        pieces = []
        for q in range(split):
            at = q * part + c * step
            piece = (hid[:, at:at + step].astype(jnp.float32) - mean) * scale
            pieces.append(piece * gain[:, at:at + step] + shift[:, at:at + step])
        rows[mine, :, LANES + c * step:LANES + (c + 1) * step] = jnp.concatenate(pieces, axis=0).astype(jnp.bfloat16)

    far_copies, mid_copies, core_copies = [], [], []
    for c in range(PARTS):
        norm_part(c)
        if c == 0:
            pl.semaphore_wait(barrier, fars + mids + cores - 3)
        here = rows.at[mine, :, spans(c)]
        far_copies.append([remote(here, here, far_s.at[c, d], far_r.at[c, d], peer) for d, peer in far_peers])

    for c in range(PARTS):
        for q in range(split):
            at = pl.ds(q * part + c * step, step)
            copy = pltpu.make_async_copy(down_hbm.at[:, at], w_down.at[:, at], down_sem.at[c, q])
            copy.start()
            down_copies.append(copy)

    tile = min(n_dev, 16)
    tiles = n_dev // tile
    tall = tile * PACK

    def over_tiles(body):
        if tiles == 1:
            body(0)
        else:
            pl.loop(0, tiles)(body)

    def row_part(shape):
        return (lax.broadcasted_iota(jnp.int32, shape, 0) // row_count) % split

    def up_part(c):
        up_copies[c].wait()

        def body(t):
            got = rows[pl.ds(t * tile, tile), :, LANES + c * step:LANES + (c + 1) * step].reshape(tall, step)
            which = row_part((tall, units))
            total = jnp.zeros((tall, units), jnp.float32)
            for q in range(split):
                piece = jnp.dot(got, w_up[q, c * step:(c + 1) * step, :], preferred_element_type=jnp.float32)
                total = total + jnp.where(which == q, piece, 0.0)
            at = pl.ds(pl.multiple_of(t * tall, tall), tall)
            if c == 0:
                acc[at, :] = total
            else:
                acc[at, :] += total

        over_tiles(body)

    for s in range(PARTS + 2):
        if s < PARTS:
            for copy in far_copies[s]:
                copy.wait_recv()
            here = rows.at[pl.ds(place(core, mid, 0), fars), :, spans(s)]
            mid_copies.append([remote(here, here, mid_s.at[s, d], mid_r.at[s, d], peer) for d, peer in mid_peers])
        if 0 <= s - 1 < PARTS:
            c = s - 1
            for copy in mid_copies[c]:
                copy.wait_recv()
            here = rows.at[pl.ds(place(core, 0, 0), fars * mids), :, spans(c)]
            core_copies.append([remote(here, here, core_s.at[c, d], core_r.at[c, d], peer) for d, peer in core_peers])
        if 0 <= s - 2:
            c = s - 2
            for copy in core_copies[c]:
                copy.wait_recv()
            up_part(c)

    def hidden_part(t):
        at = pl.ds(pl.multiple_of(t * tall, tall), tall)
        total = acc[at, :].reshape(tile, 2, 8, units)
        total = total[:, 0] + total[:, 1]
        if split == 4:
            total = total + pltpu.roll(total, row_count, 1)
        total = jnp.concatenate([total[:, None], total[:, None]], axis=1).reshape(tall, units)
        value = jnp.maximum(total + up_bias[...], 0.0)
        named = rows[pl.ds(t * tile, tile), :, 0:LANES].reshape(tall, LANES).astype(jnp.float32)
        kept = []
        for b in range(per_dev):
            wanted = (me * per_dev + b).astype(jnp.float32)
            hit = jnp.max(jnp.where(named == wanted, 1.0, 0.0), axis=1, keepdims=True)
            kept.append(jnp.where(hit > 0.0, value[:, b * BLOCK:(b + 1) * BLOCK], 0.0))
        value = jnp.concatenate(kept, axis=1)
        which = row_part((tall, units))
        for q in range(split):
            hid_cat[at, q * units:(q + 1) * units] = jnp.where(which == q, value, 0.0).astype(jnp.bfloat16)

    over_tiles(hidden_part)
    for copies in far_copies + mid_copies + core_copies:
        for copy in copies:
            copy.wait_send()

    def down_part(c):
        for q in range(split):
            down_copies[c * split + q].wait()

        def body(t):
            at = pl.ds(pl.multiple_of(t * tall, tall), tall)
            total = jnp.zeros((tall, step), jnp.float32)
            for q in range(split):
                start = q * part + c * step
                total = total + jnp.dot(hid_cat[at, q * units:(q + 1) * units], w_down[:, start:start + step],
                                        preferred_element_type=jnp.float32)
            rows[pl.ds(t * tile, tile), :, LANES + c * step:LANES + (c + 1) * step] = (
                total.astype(jnp.bfloat16).reshape(tile, PACK, step))

        over_tiles(body)

    back_core, back_mid, back_far = [], [], []
    plane = fars * mids
    for s in range(PARTS + 3):
        if s < PARTS:
            c = s
            down_part(c)
            cols = pl.ds(LANES + c * step, step)
            back_core.append([
                remote(rows.at[pl.ds(place(lax.rem(core + d, cores), 0, 0), plane), :, cols],
                       core_in.at[d - 1, :, :, pl.ds(c * step, step)], rcore_s.at[c, d], rcore_r.at[c, d], peer)
                for d, peer in core_peers])
        if 0 <= s - 1 < PARTS:
            c = s - 1
            for copy in back_core[c]:
                copy.wait_recv()
            cs = slice(c * step, (c + 1) * step)

            def chip_sum(m):
                total = rows[pl.ds(place(core, m, 0), fars), :, LANES + c * step:LANES + (c + 1) * step]
                total = total.astype(jnp.float32)
                for d in range(1, cores):
                    total = total + core_in[d - 1, pl.ds(m * fars, fars), :, cs].astype(jnp.float32)
                return total

            for d in range(1, mids):
                mid_out[d - 1, :, :, cs] = chip_sum(lax.rem(mid + d, mids)).astype(jnp.bfloat16)
            back_mid.append([
                remote(mid_out.at[d - 1, :, :, pl.ds(c * step, step)], mid_in.at[d - 1, :, :, pl.ds(c * step, step)],
                       rmid_s.at[c, d], rmid_r.at[c, d], peer)
                for d, peer in mid_peers])
            mid_own[:, :, cs] = chip_sum(mid)
        if 0 <= s - 2 < PARTS:
            c = s - 2
            for copy in back_mid[c]:
                copy.wait_recv()
            cs = slice(c * step, (c + 1) * step)

            def line_sum(f):
                total = mid_own[f, :, cs]
                for d in range(1, mids):
                    total = total + mid_in[d - 1, f, :, cs].astype(jnp.float32)
                return total

            for d in range(1, fars):
                far_out[d - 1, :, cs] = line_sum(lax.rem(far + d, fars)).astype(jnp.bfloat16)
            back_far.append([
                remote(far_out.at[d - 1, :, pl.ds(c * step, step)], far_in.at[d - 1, :, pl.ds(c * step, step)],
                       rfar_s.at[c, d], rfar_r.at[c, d], peer)
                for d, peer in far_peers])
            far_own[:, cs] = line_sum(far)
        if 0 <= s - 3:
            c = s - 3
            for copy in back_far[c]:
                copy.wait_recv()
            cs = slice(c * step, (c + 1) * step)
            total = far_own[:, cs]
            for d in range(1, fars):
                total = total + far_in[d - 1, :, cs].astype(jnp.float32)
            for q in range(split):
                at = slice(q * part + c * step, q * part + (c + 1) * step)
                mixed = hid[:, at].astype(jnp.float32) + down_bias[:, at] + total[q * row_count:(q + 1) * row_count]
                out[:, at] = mixed.astype(out.dtype)
    for copies in back_core + back_mid + back_far:
        for copy in copies:
            copy.wait_send()


def local(n_dev, hidden_in, active, ln_gain, ln_bias, up_weight, up_bias, down_weight, down_bias):
    fars, mids, cores = sizes(n_dev)
    width = hidden_in.shape[2]
    row_count = hidden_in.shape[0] * hidden_in.shape[1]
    split = PACK // row_count
    part = width // split
    units = up_weight.shape[1]
    plane = fars * mids
    vmem = pl.BlockSpec(memory_space=pltpu.VMEM)
    hbm = pl.BlockSpec(memory_space=pl.ANY)
    dma = pltpu.SemaphoreType.DMA
    bf16, f32 = jnp.bfloat16, jnp.float32
    out = pl.pallas_call(
        functools.partial(kernel, n_dev),
        out_shape=jax.ShapeDtypeStruct((row_count, width), bf16),
        in_specs=[vmem] * 6 + [hbm] * 2,
        out_specs=vmem,
        scratch_shapes=[
            pltpu.VMEM((n_dev, PACK, LANES + part), bf16),
            pltpu.VMEM((split, part, units), bf16),
            pltpu.VMEM((units, width), bf16),
            pltpu.VMEM((n_dev * PACK, units), f32),
            pltpu.VMEM((n_dev * PACK, split * units), bf16),
            pltpu.VMEM((max(cores - 1, 1), plane, PACK, part), bf16),
            pltpu.VMEM((max(mids - 1, 1), fars, PACK, part), bf16),
            pltpu.VMEM((fars, PACK, part), f32),
            pltpu.VMEM((max(mids - 1, 1), fars, PACK, part), bf16),
            pltpu.VMEM((max(fars - 1, 1), PACK, part), bf16),
            pltpu.VMEM((PACK, part), f32),
            pltpu.VMEM((max(fars - 1, 1), PACK, part), bf16),
            dma((PARTS,)), dma((PARTS, split)),
            dma((PARTS, fars)), dma((PARTS, fars)),
            dma((PARTS, mids)), dma((PARTS, mids)),
            dma((PARTS, cores)), dma((PARTS, cores)),
            dma((PARTS, cores)), dma((PARTS, cores)),
            dma((PARTS, mids)), dma((PARTS, mids)),
            dma((PARTS, fars)), dma((PARTS, fars)),
        ],
        compiler_params=pltpu.CompilerParams(
            collective_id=0, has_side_effects=True, vmem_limit_bytes=60 * 1024 * 1024),
    )(
        hidden_in.reshape(row_count, width), active.reshape(row_count, -1),
        ln_gain.reshape(1, -1), ln_bias.reshape(1, -1), up_bias.reshape(1, -1), down_bias.reshape(1, -1),
        up_weight.reshape(split, part, units), down_weight,
    )
    return out.reshape(hidden_in.shape)


def solution(mesh):
    in_specs = (
        P(None, ("groups", "tensor"), None),
        P(None, ("groups", "tensor"), None),
        P(),
        P(),
        P(None, "tensor"),
        P("tensor"),
        P("tensor", None),
        P(),
    )
    out_specs = P(None, ("groups", "tensor"), None)
    return jax.shard_map(
        functools.partial(local, mesh.shape["tensor"]), mesh=mesh, in_specs=in_specs, out_specs=out_specs,
        check_vma=False)
```

```python
import functools
import math

import jax
import jax.numpy as jnp
from jax import lax
from jax.experimental import pallas as pl
from jax.experimental.pallas import tpu as pltpu
from jax.sharding import PartitionSpec as P

BLOCK = 128
LANES = 128
PACK = 16
PARTS = 2


def sizes(n_dev):
    cores = 2 if n_dev % 2 == 0 else 1
    rest = n_dev // cores
    mids = math.isqrt(rest)
    while rest % mids:
        mids -= 1
    return rest // mids, mids, cores


def kernel(n_dev, hid, act, gain, shift, up_bias, down_bias, up_hbm, down_hbm, out,
           rows, w_up, w_down, acc, hid_cat, core_in, mid_out, mid_in, far_out, far_own, far_in,
           up_sem, down_sem, far_s, far_r, mid_s, mid_r, core_s, core_r,
           rcore_s, rcore_r, rmid_s, rmid_r, rfar_s, rfar_r):
    fars, mids, cores = sizes(n_dev)
    row_count, width = hid.shape
    split = PACK // row_count
    part = width // split
    step = part // PARTS
    units = w_up.shape[2]
    per_dev = units // BLOCK

    me = lax.axis_index("tensor")
    core = lax.rem(me, cores)
    mid = lax.rem(me // cores, mids)
    far = me // (cores * mids)

    def device(c, m, f):
        return {"tensor": (f * mids + m) * cores + c}

    def place(c, m, f):
        return (c * mids + m) * fars + f

    def other(d):
        return jnp.bitwise_xor(far, d) if fars & (fars - 1) == 0 else lax.rem(far + d, fars)

    def source(d):
        return jnp.bitwise_xor(far, d) if fars & (fars - 1) == 0 else lax.rem(far + fars - d, fars)

    far_peers = [(d, device(core, mid, other(d))) for d in range(1, fars)]
    mid_peers = [(d, device(core, lax.rem(mid + d, mids), far)) for d in range(1, mids)]
    core_peers = [(d, device(lax.rem(core + d, cores), mid, far)) for d in range(1, cores)]
    barrier = pltpu.get_barrier_semaphore()
    for _, peer in far_peers + mid_peers + core_peers:
        pl.semaphore_signal(barrier, inc=1, device_id=peer, device_id_type=pl.DeviceIdType.MESH)

    up_copies, down_copies = [], []
    for c in range(PARTS):
        copy = pltpu.make_async_copy(
            up_hbm.at[:, pl.ds(c * step, step), :], w_up.at[:, pl.ds(c * step, step), :], up_sem.at[c])
        copy.start()
        up_copies.append(copy)

    def remote(src, dst, send, recv, peer):
        copy = pltpu.make_async_remote_copy(
            src_ref=src, dst_ref=dst, send_sem=send, recv_sem=recv,
            device_id=peer, device_id_type=pl.DeviceIdType.MESH)
        copy.start()
        return copy

    x = hid[...].astype(jnp.float32)
    mean = jnp.mean(x, axis=-1, keepdims=True)
    center = x - mean
    scale = lax.rsqrt(jnp.mean(center * center, axis=-1, keepdims=True) + 1e-05)

    mine = place(core, mid, far)
    lane = lax.broadcasted_iota(jnp.int32, (row_count, LANES), 1)
    ids = jnp.full((row_count, LANES), -1, jnp.int32)
    for a in range(act.shape[1]):
        ids = jnp.where(lane == a, act[:, a:a + 1], ids)
    ids = ids.astype(jnp.float32)
    rows[mine, :, 0:LANES] = jnp.concatenate([ids] * split, axis=0).astype(jnp.bfloat16)

    def spans(c):
        start = 0 if c == 0 else LANES + c * step
        return pl.ds(start, step + (LANES if c == 0 else 0))

    def norm_part(c):
        pieces = []
        for q in range(split):
            at = q * part + c * step
            piece = (hid[:, at:at + step].astype(jnp.float32) - mean) * scale
            pieces.append(piece * gain[:, at:at + step] + shift[:, at:at + step])
        rows[mine, :, LANES + c * step:LANES + (c + 1) * step] = jnp.concatenate(pieces, axis=0).astype(jnp.bfloat16)

    def spread(c, d):
        here = rows.at[place(core, mid, source(d) if d else far), :, spans(c)]
        return [remote(here, here, mid_s.at[c, d, e], mid_r.at[c, d, e], peer) for e, peer in mid_peers]

    far_copies, mid_copies, core_copies = [], [[] for _ in range(PARTS)], []
    for c in range(PARTS):
        norm_part(c)
        if c == 0:
            pl.semaphore_wait(barrier, fars + mids + cores - 3)
        mid_copies[c] += spread(c, 0)
        here = rows.at[mine, :, spans(c)]
        far_copies.append([remote(here, here, far_s.at[c, d], far_r.at[c, d], peer) for d, peer in far_peers])

    for c in range(PARTS):
        for q in range(split):
            at = pl.ds(q * part + c * step, step)
            copy = pltpu.make_async_copy(down_hbm.at[:, at], w_down.at[:, at], down_sem.at[c, q])
            copy.start()
            down_copies.append(copy)

    tile = min(n_dev, 16)
    tiles = n_dev // tile
    tall = tile * PACK

    def over_tiles(body):
        if tiles == 1:
            body(0)
        else:
            pl.loop(0, tiles)(body)

    def row_part(shape):
        return (lax.broadcasted_iota(jnp.int32, shape, 0) // row_count) % split

    def up_part(c):
        up_copies[c].wait()

        def body(t):
            got = rows[pl.ds(t * tile, tile), :, LANES + c * step:LANES + (c + 1) * step].reshape(tall, step)
            which = row_part((tall, units))
            total = jnp.zeros((tall, units), jnp.float32)
            for q in range(split):
                piece = jnp.dot(got, w_up[q, c * step:(c + 1) * step, :], preferred_element_type=jnp.float32)
                total = total + jnp.where(which == q, piece, 0.0)
            at = pl.ds(pl.multiple_of(t * tall, tall), tall)
            if c == 0:
                acc[at, :] = total
            else:
                acc[at, :] += total

        over_tiles(body)

    for c in range(PARTS):
        for d in range(1, fars):
            far_copies[c][d - 1].wait_recv()
            mid_copies[c] += spread(c, d)
    for c in range(PARTS):
        for copy in mid_copies[c]:
            copy.wait_recv()
        here = rows.at[pl.ds(place(core, 0, 0), fars * mids), :, spans(c)]
        core_copies.append([remote(here, here, core_s.at[c, d], core_r.at[c, d], peer) for d, peer in core_peers])
        for copy in core_copies[c]:
            copy.wait_recv()
        up_part(c)

    def hidden_part(t):
        at = pl.ds(pl.multiple_of(t * tall, tall), tall)
        total = acc[at, :].reshape(tile, 2, 8, units)
        total = total[:, 0] + total[:, 1]
        if split == 4:
            total = total + pltpu.roll(total, row_count, 1)
        total = jnp.concatenate([total[:, None], total[:, None]], axis=1).reshape(tall, units)
        value = jnp.maximum(total + up_bias[...], 0.0)
        named = rows[pl.ds(t * tile, tile), :, 0:LANES].reshape(tall, LANES).astype(jnp.float32)
        kept = []
        for b in range(per_dev):
            wanted = (me * per_dev + b).astype(jnp.float32)
            hit = jnp.max(jnp.where(named == wanted, 1.0, 0.0), axis=1, keepdims=True)
            kept.append(jnp.where(hit > 0.0, value[:, b * BLOCK:(b + 1) * BLOCK], 0.0))
        value = jnp.concatenate(kept, axis=1)
        which = row_part((tall, units))
        for q in range(split):
            hid_cat[at, q * units:(q + 1) * units] = jnp.where(which == q, value, 0.0).astype(jnp.bfloat16)

    over_tiles(hidden_part)
    for copies in far_copies + mid_copies + core_copies:
        for copy in copies:
            copy.wait_send()

    def down_part(c):
        for q in range(split):
            down_copies[c * split + q].wait()

        def body(t):
            at = pl.ds(pl.multiple_of(t * tall, tall), tall)
            total = jnp.zeros((tall, step), jnp.float32)
            for q in range(split):
                start = q * part + c * step
                total = total + jnp.dot(hid_cat[at, q * units:(q + 1) * units], w_down[:, start:start + step],
                                        preferred_element_type=jnp.float32)
            rows[pl.ds(t * tile, tile), :, LANES + c * step:LANES + (c + 1) * step] = (
                total.astype(jnp.bfloat16).reshape(tile, PACK, step))

        over_tiles(body)

    back_core, back_mid, back_far = [], {}, []
    plane = fars * mids

    def chip_sum(c, m, f):
        at = slice(c * step, (c + 1) * step)
        total = rows[place(core, m, f), :, LANES + c * step:LANES + (c + 1) * step].astype(jnp.float32)
        for e in range(1, cores):
            total = total + core_in[e - 1, m * fars + f, :, at].astype(jnp.float32)
        return total

    def send_mid(c, d):
        at = slice(c * step, (c + 1) * step)
        for e, peer in mid_peers:
            mid_out[e - 1, d, :, at] = chip_sum(c, lax.rem(mid + e, mids), other(d) if d else far).astype(jnp.bfloat16)
            cols = pl.ds(c * step, step)
            back_mid[c, d, e] = remote(mid_out.at[e - 1, d, :, cols], mid_in.at[e - 1, d, :, cols],
                                       rmid_s.at[c, d, e], rmid_r.at[c, d, e], peer)

    def line_sum(c, d):
        total = chip_sum(c, mid, other(d) if d else far)
        for e in range(1, mids):
            back_mid[c, d, e].wait_recv()
            total = total + mid_in[e - 1, d, :, c * step:(c + 1) * step].astype(jnp.float32)
        return total

    for c in range(PARTS):
        down_part(c)
        cols = pl.ds(LANES + c * step, step)
        back_core.append([
            remote(rows.at[pl.ds(place(lax.rem(core + d, cores), 0, 0), plane), :, cols],
                   core_in.at[d - 1, :, :, pl.ds(c * step, step)], rcore_s.at[c, d], rcore_r.at[c, d], peer)
            for d, peer in core_peers])
    for c in range(PARTS):
        for copy in back_core[c]:
            copy.wait_recv()
        for d in range(1, fars):
            send_mid(c, d)
    for c in range(PARTS):
        send_mid(c, 0)
    for c in range(PARTS):
        cs = slice(c * step, (c + 1) * step)
        for d, peer in far_peers:
            far_out[d - 1, :, cs] = line_sum(c, d).astype(jnp.bfloat16)
            cols = pl.ds(c * step, step)
            back_far.append(remote(far_out.at[d - 1, :, cols], far_in.at[d - 1, :, cols],
                                   rfar_s.at[c, d], rfar_r.at[c, d], peer))
    for c in range(PARTS):
        cs = slice(c * step, (c + 1) * step)
        far_own[:, cs] = line_sum(c, 0)
    for c in range(PARTS):
        cs = slice(c * step, (c + 1) * step)
        total = far_own[:, cs]
        for d in range(1, fars):
            back_far[c * (fars - 1) + d - 1].wait_recv()
            total = total + far_in[d - 1, :, cs].astype(jnp.float32)
        for q in range(split):
            at = slice(q * part + c * step, q * part + (c + 1) * step)
            mixed = hid[:, at].astype(jnp.float32) + down_bias[:, at] + total[q * row_count:(q + 1) * row_count]
            out[:, at] = mixed.astype(out.dtype)
    for copies in back_core + [back_mid.values(), back_far]:
        for copy in copies:
            copy.wait_send()


def local(n_dev, hidden_in, active, ln_gain, ln_bias, up_weight, up_bias, down_weight, down_bias):
    fars, mids, cores = sizes(n_dev)
    width = hidden_in.shape[2]
    row_count = hidden_in.shape[0] * hidden_in.shape[1]
    split = PACK // row_count
    part = width // split
    units = up_weight.shape[1]
    plane = fars * mids
    vmem = pl.BlockSpec(memory_space=pltpu.VMEM)
    hbm = pl.BlockSpec(memory_space=pl.ANY)
    dma = pltpu.SemaphoreType.DMA
    bf16, f32 = jnp.bfloat16, jnp.float32
    out = pl.pallas_call(
        functools.partial(kernel, n_dev),
        out_shape=jax.ShapeDtypeStruct((row_count, width), bf16),
        in_specs=[vmem] * 6 + [hbm] * 2,
        out_specs=vmem,
        scratch_shapes=[
            pltpu.VMEM((n_dev, PACK, LANES + part), bf16),
            pltpu.VMEM((split, part, units), bf16),
            pltpu.VMEM((units, width), bf16),
            pltpu.VMEM((n_dev * PACK, units), f32),
            pltpu.VMEM((n_dev * PACK, split * units), bf16),
            pltpu.VMEM((max(cores - 1, 1), plane, PACK, part), bf16),
            pltpu.VMEM((max(mids - 1, 1), fars, PACK, part), bf16),
            pltpu.VMEM((max(mids - 1, 1), fars, PACK, part), bf16),
            pltpu.VMEM((max(fars - 1, 1), PACK, part), bf16),
            pltpu.VMEM((PACK, part), f32),
            pltpu.VMEM((max(fars - 1, 1), PACK, part), bf16),
            dma((PARTS,)), dma((PARTS, split)),
            dma((PARTS, fars)), dma((PARTS, fars)),
            dma((PARTS, fars, mids)), dma((PARTS, fars, mids)),
            dma((PARTS, cores)), dma((PARTS, cores)),
            dma((PARTS, cores)), dma((PARTS, cores)),
            dma((PARTS, fars, mids)), dma((PARTS, fars, mids)),
            dma((PARTS, fars)), dma((PARTS, fars)),
        ],
        compiler_params=pltpu.CompilerParams(
            collective_id=0, has_side_effects=True, vmem_limit_bytes=60 * 1024 * 1024),
    )(
        hidden_in.reshape(row_count, width), active.reshape(row_count, -1),
        ln_gain.reshape(1, -1), ln_bias.reshape(1, -1), up_bias.reshape(1, -1), down_bias.reshape(1, -1),
        up_weight.reshape(split, part, units), down_weight,
    )
    return out.reshape(hidden_in.shape)


def solution(mesh):
    in_specs = (
        P(None, ("groups", "tensor"), None),
        P(None, ("groups", "tensor"), None),
        P(),
        P(),
        P(None, "tensor"),
        P("tensor"),
        P("tensor", None),
        P(),
    )
    out_specs = P(None, ("groups", "tensor"), None)
    return jax.shard_map(
        functools.partial(local, mesh.shape["tensor"]), mesh=mesh, in_specs=in_specs, out_specs=out_specs,
        check_vma=False)
```

```python
import functools
import math

import jax
import jax.numpy as jnp
from jax import lax
from jax.experimental import pallas as pl
from jax.experimental.pallas import tpu as pltpu
from jax.sharding import PartitionSpec as P

BLOCK = 128
LANES = 128
PACK = 16
PARTS = 2


def sizes(n_dev):
    cores = 2 if n_dev % 2 == 0 else 1
    rest = n_dev // cores
    mids = math.isqrt(rest)
    while rest % mids:
        mids -= 1
    return rest // mids, mids, cores


def kernel(n_dev, hid, act, gain, shift, up_bias, down_bias, up_hbm, down_hbm, out,
           rows, w_up, w_down, acc, hid_cat, core_in, mid_out, mid_in, far_out, far_own, far_in,
           up_sem, down_sem, far_s, far_r, mid_s, mid_r, core_s, core_r,
           rcore_s, rcore_r, rmid_s, rmid_r, rfar_s, rfar_r):
    fars, mids, cores = sizes(n_dev)
    row_count, width = hid.shape
    split = PACK // row_count
    part = width // split
    step = part // PARTS
    units = w_up.shape[2]
    per_dev = units // BLOCK

    me = lax.axis_index("tensor")
    core = lax.rem(me, cores)
    mid = lax.rem(me // cores, mids)
    far = me // (cores * mids)

    def device(c, m, f):
        return {"tensor": (f * mids + m) * cores + c}

    def place(c, m, f):
        return (c * mids + m) * fars + f

    def other(d):
        return jnp.bitwise_xor(far, d) if fars & (fars - 1) == 0 else lax.rem(far + d, fars)

    def source(d):
        return jnp.bitwise_xor(far, d) if fars & (fars - 1) == 0 else lax.rem(far + fars - d, fars)

    order = list(range(1, fars))
    back_order = list(range(2, fars)) + [1] if fars > 1 else []
    far_peers = [(d, device(core, mid, other(d))) for d in order]
    mid_peers = [(d, device(core, lax.rem(mid + d, mids), far)) for d in range(1, mids)]
    core_peers = [(d, device(lax.rem(core + d, cores), mid, far)) for d in range(1, cores)]
    barrier = pltpu.get_barrier_semaphore()
    for _, peer in far_peers + mid_peers + core_peers:
        pl.semaphore_signal(barrier, inc=1, device_id=peer, device_id_type=pl.DeviceIdType.MESH)

    up_copies, down_copies = [], []
    for c in range(PARTS):
        copy = pltpu.make_async_copy(
            up_hbm.at[:, pl.ds(c * step, step), :], w_up.at[:, pl.ds(c * step, step), :], up_sem.at[c])
        copy.start()
        up_copies.append(copy)

    def remote(src, dst, send, recv, peer):
        copy = pltpu.make_async_remote_copy(
            src_ref=src, dst_ref=dst, send_sem=send, recv_sem=recv,
            device_id=peer, device_id_type=pl.DeviceIdType.MESH)
        copy.start()
        return copy

    x = hid[...].astype(jnp.float32)
    mean = jnp.mean(x, axis=-1, keepdims=True)
    center = x - mean
    scale = lax.rsqrt(jnp.mean(center * center, axis=-1, keepdims=True) + 1e-05)

    mine = place(core, mid, far)
    lane = lax.broadcasted_iota(jnp.int32, (row_count, LANES), 1)
    ids = jnp.full((row_count, LANES), -1, jnp.int32)
    for a in range(act.shape[1]):
        ids = jnp.where(lane == a, act[:, a:a + 1], ids)
    ids = ids.astype(jnp.float32)
    rows[mine, :, 0:LANES] = jnp.concatenate([ids] * split, axis=0).astype(jnp.bfloat16)

    def spans(c):
        start = 0 if c == 0 else LANES + c * step
        return pl.ds(start, step + (LANES if c == 0 else 0))

    def norm_part(c):
        pieces = []
        for q in range(split):
            at = q * part + c * step
            piece = (hid[:, at:at + step].astype(jnp.float32) - mean) * scale
            pieces.append(piece * gain[:, at:at + step] + shift[:, at:at + step])
        rows[mine, :, LANES + c * step:LANES + (c + 1) * step] = jnp.concatenate(pieces, axis=0).astype(jnp.bfloat16)

    def spread(c, d):
        here = rows.at[place(core, mid, source(d) if d else far), :, spans(c)]
        return [remote(here, here, mid_s.at[c, d, e], mid_r.at[c, d, e], peer) for e, peer in mid_peers]

    far_copies, mid_copies, core_copies = [], [[] for _ in range(PARTS)], [[] for _ in range(PARTS)]
    for c in range(PARTS):
        norm_part(c)
        if c == 0:
            pl.semaphore_wait(barrier, fars + mids + cores - 3)
        mid_copies[c] += spread(c, 0)
        here = rows.at[mine, :, spans(c)]
        far_copies.append({d: remote(here, here, far_s.at[c, d], far_r.at[c, d], peer) for d, peer in far_peers})

    for c in range(PARTS):
        for q in range(split):
            at = pl.ds(q * part + c * step, step)
            copy = pltpu.make_async_copy(down_hbm.at[:, at], w_down.at[:, at], down_sem.at[c, q])
            copy.start()
            down_copies.append(copy)

    tile = min(n_dev, 16)
    tiles = n_dev // tile
    tall = tile * PACK

    def over_tiles(body):
        if tiles == 1:
            body(0)
        else:
            pl.loop(0, tiles)(body)

    def row_part(shape):
        return (lax.broadcasted_iota(jnp.int32, shape, 0) // row_count) % split

    def up_part(c):
        up_copies[c].wait()

        def body(t):
            got = rows[pl.ds(t * tile, tile), :, LANES + c * step:LANES + (c + 1) * step].reshape(tall, step)
            which = row_part((tall, units))
            total = jnp.zeros((tall, units), jnp.float32)
            for q in range(split):
                piece = jnp.dot(got, w_up[q, c * step:(c + 1) * step, :], preferred_element_type=jnp.float32)
                total = total + jnp.where(which == q, piece, 0.0)
            at = pl.ds(pl.multiple_of(t * tall, tall), tall)
            if c == 0:
                acc[at, :] = total
            else:
                acc[at, :] += total

        over_tiles(body)

    def share(c, e):
        here = rows.at[pl.ds(place(core, lax.rem(mid + e, mids), 0), fars), :, spans(c)]
        return [remote(here, here, core_s.at[c, e, d], core_r.at[c, e, d], peer) for d, peer in core_peers]

    for c in range(PARTS):
        for d in order:
            far_copies[c][d].wait_recv()
            mid_copies[c] += spread(c, d)
        core_copies[c] += share(c, 0)
    for c in range(PARTS):
        for copy in mid_copies[c]:
            copy.wait_recv()
        for e in range(1, mids):
            core_copies[c] += share(c, e)
        for copy in core_copies[c]:
            copy.wait_recv()
        up_part(c)

    def hidden_part(t):
        at = pl.ds(pl.multiple_of(t * tall, tall), tall)
        total = acc[at, :].reshape(tile, 2, 8, units)
        total = total[:, 0] + total[:, 1]
        if split == 4:
            total = total + pltpu.roll(total, row_count, 1)
        total = jnp.concatenate([total[:, None], total[:, None]], axis=1).reshape(tall, units)
        value = jnp.maximum(total + up_bias[...], 0.0)
        named = rows[pl.ds(t * tile, tile), :, 0:LANES].reshape(tall, LANES).astype(jnp.float32)
        kept = []
        for b in range(per_dev):
            wanted = (me * per_dev + b).astype(jnp.float32)
            hit = jnp.max(jnp.where(named == wanted, 1.0, 0.0), axis=1, keepdims=True)
            kept.append(jnp.where(hit > 0.0, value[:, b * BLOCK:(b + 1) * BLOCK], 0.0))
        value = jnp.concatenate(kept, axis=1)
        which = row_part((tall, units))
        for q in range(split):
            hid_cat[at, q * units:(q + 1) * units] = jnp.where(which == q, value, 0.0).astype(jnp.bfloat16)

    over_tiles(hidden_part)
    for copies in [list(got.values()) for got in far_copies] + mid_copies + core_copies:
        for copy in copies:
            copy.wait_send()

    def down_part(c):
        for q in range(split):
            down_copies[c * split + q].wait()

        def body(t):
            at = pl.ds(pl.multiple_of(t * tall, tall), tall)
            total = jnp.zeros((tall, step), jnp.float32)
            for q in range(split):
                start = q * part + c * step
                total = total + jnp.dot(hid_cat[at, q * units:(q + 1) * units], w_down[:, start:start + step],
                                        preferred_element_type=jnp.float32)
            rows[pl.ds(t * tile, tile), :, LANES + c * step:LANES + (c + 1) * step] = (
                total.astype(jnp.bfloat16).reshape(tile, PACK, step))

        over_tiles(body)

    back_core, back_mid, back_far = {}, {}, {}

    def chip_sum(c, m, f):
        at = slice(c * step, (c + 1) * step)
        total = rows[place(core, m, f), :, LANES + c * step:LANES + (c + 1) * step].astype(jnp.float32)
        for e in range(1, cores):
            total = total + core_in[e - 1, m * fars + f, :, at].astype(jnp.float32)
        return total

    def send_mid(c, d):
        at = slice(c * step, (c + 1) * step)
        for e, peer in mid_peers:
            mid_out[e - 1, d, :, at] = chip_sum(c, lax.rem(mid + e, mids), other(d) if d else far).astype(jnp.bfloat16)
            cols = pl.ds(c * step, step)
            back_mid[c, d, e] = remote(mid_out.at[e - 1, d, :, cols], mid_in.at[e - 1, d, :, cols],
                                       rmid_s.at[c, d, e], rmid_r.at[c, d, e], peer)

    def line_sum(c, d):
        total = chip_sum(c, mid, other(d) if d else far)
        for e in range(1, mids):
            back_mid[c, d, e].wait_recv()
            total = total + mid_in[e - 1, d, :, c * step:(c + 1) * step].astype(jnp.float32)
        return total

    for c in range(PARTS):
        down_part(c)
        for e in list(range(1, mids)) + [0]:
            m = lax.rem(mid + e, mids)
            for d, peer in core_peers:
                back_core[c, e, d] = remote(
                    rows.at[pl.ds(place(lax.rem(core + d, cores), m, 0), fars), :, pl.ds(LANES + c * step, step)],
                    core_in.at[d - 1, pl.ds(m * fars, fars), :, pl.ds(c * step, step)],
                    rcore_s.at[c, e, d], rcore_r.at[c, e, d], peer)
    for c in range(PARTS):
        for e in range(1, mids):
            for d in range(1, cores):
                back_core[c, e, d].wait_recv()
        for d in back_order:
            send_mid(c, d)
    for c in range(PARTS):
        send_mid(c, 0)
    for c in range(PARTS):
        for d in range(1, cores):
            back_core[c, 0, d].wait_recv()
    for c in range(PARTS):
        cs = slice(c * step, (c + 1) * step)
        for d in back_order:
            peer = device(core, mid, other(d))
            far_out[d - 1, :, cs] = line_sum(c, d).astype(jnp.bfloat16)
            cols = pl.ds(c * step, step)
            back_far[c, d] = remote(far_out.at[d - 1, :, cols], far_in.at[d - 1, :, cols],
                                    rfar_s.at[c, d], rfar_r.at[c, d], peer)
    for c in range(PARTS):
        cs = slice(c * step, (c + 1) * step)
        far_own[:, cs] = line_sum(c, 0)
    for c in range(PARTS):
        cs = slice(c * step, (c + 1) * step)
        total = far_own[:, cs]
        for d in range(1, fars):
            back_far[c, d].wait_recv()
            total = total + far_in[d - 1, :, cs].astype(jnp.float32)
        for q in range(split):
            at = slice(q * part + c * step, q * part + (c + 1) * step)
            mixed = hid[:, at].astype(jnp.float32) + down_bias[:, at] + total[q * row_count:(q + 1) * row_count]
            out[:, at] = mixed.astype(out.dtype)
    for copies in [back_core.values(), back_mid.values(), back_far.values()]:
        for copy in copies:
            copy.wait_send()


def local(n_dev, hidden_in, active, ln_gain, ln_bias, up_weight, up_bias, down_weight, down_bias):
    fars, mids, cores = sizes(n_dev)
    width = hidden_in.shape[2]
    row_count = hidden_in.shape[0] * hidden_in.shape[1]
    split = PACK // row_count
    part = width // split
    units = up_weight.shape[1]
    plane = fars * mids
    vmem = pl.BlockSpec(memory_space=pltpu.VMEM)
    hbm = pl.BlockSpec(memory_space=pl.ANY)
    dma = pltpu.SemaphoreType.DMA
    bf16, f32 = jnp.bfloat16, jnp.float32
    out = pl.pallas_call(
        functools.partial(kernel, n_dev),
        out_shape=jax.ShapeDtypeStruct((row_count, width), bf16),
        in_specs=[vmem] * 6 + [hbm] * 2,
        out_specs=vmem,
        scratch_shapes=[
            pltpu.VMEM((n_dev, PACK, LANES + part), bf16),
            pltpu.VMEM((split, part, units), bf16),
            pltpu.VMEM((units, width), bf16),
            pltpu.VMEM((n_dev * PACK, units), f32),
            pltpu.VMEM((n_dev * PACK, split * units), bf16),
            pltpu.VMEM((max(cores - 1, 1), plane, PACK, part), bf16),
            pltpu.VMEM((max(mids - 1, 1), fars, PACK, part), bf16),
            pltpu.VMEM((max(mids - 1, 1), fars, PACK, part), bf16),
            pltpu.VMEM((max(fars - 1, 1), PACK, part), bf16),
            pltpu.VMEM((PACK, part), f32),
            pltpu.VMEM((max(fars - 1, 1), PACK, part), bf16),
            dma((PARTS,)), dma((PARTS, split)),
            dma((PARTS, fars)), dma((PARTS, fars)),
            dma((PARTS, fars, mids)), dma((PARTS, fars, mids)),
            dma((PARTS, mids, cores)), dma((PARTS, mids, cores)),
            dma((PARTS, mids, cores)), dma((PARTS, mids, cores)),
            dma((PARTS, fars, mids)), dma((PARTS, fars, mids)),
            dma((PARTS, fars)), dma((PARTS, fars)),
        ],
        compiler_params=pltpu.CompilerParams(
            collective_id=0, has_side_effects=True, vmem_limit_bytes=60 * 1024 * 1024),
    )(
        hidden_in.reshape(row_count, width), active.reshape(row_count, -1),
        ln_gain.reshape(1, -1), ln_bias.reshape(1, -1), up_bias.reshape(1, -1), down_bias.reshape(1, -1),
        up_weight.reshape(split, part, units), down_weight,
    )
    return out.reshape(hidden_in.shape)


def solution(mesh):
    in_specs = (
        P(None, ("groups", "tensor"), None),
        P(None, ("groups", "tensor"), None),
        P(),
        P(),
        P(None, "tensor"),
        P("tensor"),
        P("tensor", None),
        P(),
    )
    out_specs = P(None, ("groups", "tensor"), None)
    return jax.shard_map(
        functools.partial(local, mesh.shape["tensor"]), mesh=mesh, in_specs=in_specs, out_specs=out_specs,
        check_vma=False)
```

```python
import functools
import math

import jax
import jax.numpy as jnp
from jax import lax
from jax.experimental import pallas as pl
from jax.experimental.pallas import tpu as pltpu
from jax.sharding import PartitionSpec as P

BLOCK = 128
LANES = 128
PACK = 16
PARTS = 2


def sizes(n_dev):
    cores = 2 if n_dev % 2 == 0 else 1
    rest = n_dev // cores
    mids = math.isqrt(rest)
    while rest % mids:
        mids -= 1
    return rest // mids, mids, cores


def kernel(n_dev, hid, act, gain, shift, up_bias, down_bias, up_hbm, down_hbm, out,
           rows, w_up, w_down, acc, hid_cat, core_in, mid_out, mid_in, far_out, far_own, far_in,
           up_sem, down_sem, far_s, far_r, mid_s, mid_r, core_s, core_r,
           rcore_s, rcore_r, rmid_s, rmid_r, rfar_s, rfar_r):
    fars, mids, cores = sizes(n_dev)
    row_count, width = hid.shape
    split = PACK // row_count
    part = width // split
    step = part // PARTS
    units = w_up.shape[2]
    per_dev = units // BLOCK

    me = lax.axis_index("tensor")
    core = lax.rem(me, cores)
    mid = lax.rem(me // cores, mids)
    far = me // (cores * mids)

    def device(c, m, f):
        return {"tensor": (f * mids + m) * cores + c}

    def place(c, m, f):
        return (c * mids + m) * fars + f

    def other(d):
        return jnp.bitwise_xor(far, d) if fars & (fars - 1) == 0 else lax.rem(far + d, fars)

    def source(d):
        return jnp.bitwise_xor(far, d) if fars & (fars - 1) == 0 else lax.rem(far + fars - d, fars)

    order = list(range(1, fars))
    back_order = list(range(2, fars)) + [1] if fars > 1 else []
    far_peers = [(d, device(core, mid, other(d))) for d in order]
    mid_peers = [(d, device(core, lax.rem(mid + d, mids), far)) for d in range(1, mids)]
    core_peers = [(d, device(lax.rem(core + d, cores), mid, far)) for d in range(1, cores)]
    barrier = pltpu.get_barrier_semaphore()
    for _, peer in far_peers + mid_peers + core_peers:
        pl.semaphore_signal(barrier, inc=1, device_id=peer, device_id_type=pl.DeviceIdType.MESH)

    up_copies, down_copies = [], []
    for c in range(PARTS):
        copy = pltpu.make_async_copy(
            up_hbm.at[:, pl.ds(c * step, step), :], w_up.at[:, pl.ds(c * step, step), :], up_sem.at[c])
        copy.start()
        up_copies.append(copy)

    def remote(src, dst, send, recv, peer):
        copy = pltpu.make_async_remote_copy(
            src_ref=src, dst_ref=dst, send_sem=send, recv_sem=recv,
            device_id=peer, device_id_type=pl.DeviceIdType.MESH)
        copy.start()
        return copy

    x = hid[...].astype(jnp.float32)
    mean = jnp.mean(x, axis=-1, keepdims=True)
    center = x - mean
    scale = lax.rsqrt(jnp.mean(center * center, axis=-1, keepdims=True) + 1e-05)

    mine = place(core, mid, far)
    lane = lax.broadcasted_iota(jnp.int32, (row_count, LANES), 1)
    ids = jnp.full((row_count, LANES), -1, jnp.int32)
    for a in range(act.shape[1]):
        ids = jnp.where(lane == a, act[:, a:a + 1], ids)
    ids = ids.astype(jnp.float32)
    rows[mine, :, 0:LANES] = jnp.concatenate([ids] * split, axis=0).astype(jnp.bfloat16)

    def spans(c):
        start = 0 if c == 0 else LANES + c * step
        return pl.ds(start, step + (LANES if c == 0 else 0))

    def norm_part(c):
        pieces = []
        for q in range(split):
            at = q * part + c * step
            piece = (hid[:, at:at + step].astype(jnp.float32) - mean) * scale
            pieces.append(piece * gain[:, at:at + step] + shift[:, at:at + step])
        rows[mine, :, LANES + c * step:LANES + (c + 1) * step] = jnp.concatenate(pieces, axis=0).astype(jnp.bfloat16)

    def spread(c, d):
        here = rows.at[place(core, mid, source(d) if d else far), :, spans(c)]
        return [remote(here, here, mid_s.at[c, d, e], mid_r.at[c, d, e], peer) for e, peer in mid_peers]

    far_copies, mid_copies, core_copies = [], [[] for _ in range(PARTS)], [[] for _ in range(PARTS)]
    for c in range(PARTS):
        norm_part(c)
        if c == 0:
            pl.semaphore_wait(barrier, fars + mids + cores - 3)
        mid_copies[c] += spread(c, 0)
        here = rows.at[mine, :, spans(c)]
        far_copies.append({d: remote(here, here, far_s.at[c, d], far_r.at[c, d], peer) for d, peer in far_peers})

    for c in range(PARTS):
        for q in range(split):
            at = pl.ds(q * part + c * step, step)
            copy = pltpu.make_async_copy(down_hbm.at[:, at], w_down.at[:, at], down_sem.at[c, q])
            copy.start()
            down_copies.append(copy)

    tile = min(n_dev, 16)
    tiles = n_dev // tile
    tall = tile * PACK

    def over_tiles(body):
        if tiles == 1:
            body(0)
        else:
            pl.loop(0, tiles)(body)

    def row_part(shape):
        return (lax.broadcasted_iota(jnp.int32, shape, 0) // row_count) % split

    def up_part(c):
        up_copies[c].wait()

        def body(t):
            got = rows[pl.ds(t * tile, tile), :, LANES + c * step:LANES + (c + 1) * step].reshape(tall, step)
            which = row_part((tall, units))
            total = jnp.zeros((tall, units), jnp.float32)
            for q in range(split):
                piece = jnp.dot(got, w_up[q, c * step:(c + 1) * step, :], preferred_element_type=jnp.float32)
                total = total + jnp.where(which == q, piece, 0.0)
            at = pl.ds(pl.multiple_of(t * tall, tall), tall)
            if c == 0:
                acc[at, :] = total
            else:
                acc[at, :] += total

        over_tiles(body)

    def share(c, e):
        here = rows.at[pl.ds(place(core, lax.rem(mid + e, mids), 0), fars), :, spans(c)]
        return [remote(here, here, core_s.at[c, e, d], core_r.at[c, e, d], peer) for d, peer in core_peers]

    for c in range(PARTS):
        for d in order:
            far_copies[c][d].wait_recv()
            mid_copies[c] += spread(c, d)
        core_copies[c] += share(c, 0)
    for c in range(PARTS):
        for copy in mid_copies[c]:
            copy.wait_recv()
        for e in range(1, mids):
            core_copies[c] += share(c, e)
        for copy in core_copies[c]:
            copy.wait_recv()
        up_part(c)

    def hidden_part(t):
        at = pl.ds(pl.multiple_of(t * tall, tall), tall)
        total = acc[at, :].reshape(tile, 2, 8, units)
        total = total[:, 0] + total[:, 1]
        if split == 4:
            total = total + pltpu.roll(total, row_count, 1)
        total = jnp.concatenate([total[:, None], total[:, None]], axis=1).reshape(tall, units)
        value = jnp.maximum(total + up_bias[...], 0.0)
        named = rows[pl.ds(t * tile, tile), :, 0:LANES].reshape(tall, LANES).astype(jnp.float32)
        kept = []
        for b in range(per_dev):
            wanted = (me * per_dev + b).astype(jnp.float32)
            hit = jnp.max(jnp.where(named == wanted, 1.0, 0.0), axis=1, keepdims=True)
            kept.append(jnp.where(hit > 0.0, value[:, b * BLOCK:(b + 1) * BLOCK], 0.0))
        value = jnp.concatenate(kept, axis=1)
        which = row_part((tall, units))
        for q in range(split):
            hid_cat[at, q * units:(q + 1) * units] = jnp.where(which == q, value, 0.0).astype(jnp.bfloat16)

    over_tiles(hidden_part)
    for copies in [list(got.values()) for got in far_copies] + mid_copies + core_copies:
        for copy in copies:
            copy.wait_send()

    def down_part(c):
        for q in range(split):
            down_copies[c * split + q].wait()

        def body(t):
            at = pl.ds(pl.multiple_of(t * tall, tall), tall)
            total = jnp.zeros((tall, step), jnp.float32)
            for q in range(split):
                start = q * part + c * step
                total = total + jnp.dot(hid_cat[at, q * units:(q + 1) * units], w_down[:, start:start + step],
                                        preferred_element_type=jnp.float32)
            rows[pl.ds(t * tile, tile), :, LANES + c * step:LANES + (c + 1) * step] = (
                total.astype(jnp.bfloat16).reshape(tile, PACK, step))

        over_tiles(body)

    back_core, back_mid, back_far = {}, {}, {}

    def chip_sum(c, m, f):
        at = slice(c * step, (c + 1) * step)
        total = rows[place(core, m, f), :, LANES + c * step:LANES + (c + 1) * step].astype(jnp.float32)
        for e in range(1, cores):
            total = total + core_in[e - 1, m * fars + f, :, at].astype(jnp.float32)
        return total

    def send_mid(c, d):
        at = slice(c * step, (c + 1) * step)
        for e, peer in mid_peers:
            mid_out[e - 1, d, :, at] = chip_sum(c, lax.rem(mid + e, mids), other(d) if d else far).astype(jnp.bfloat16)
            cols = pl.ds(c * step, step)
            back_mid[c, d, e] = remote(mid_out.at[e - 1, d, :, cols], mid_in.at[e - 1, d, :, cols],
                                       rmid_s.at[c, d, e], rmid_r.at[c, d, e], peer)

    def line_sum(c, d):
        total = chip_sum(c, mid, other(d) if d else far)
        for e in range(1, mids):
            back_mid[c, d, e].wait_recv()
            total = total + mid_in[e - 1, d, :, c * step:(c + 1) * step].astype(jnp.float32)
        return total

    for c in range(PARTS):
        down_part(c)
        for e in list(range(1, mids)) + [0]:
            m = lax.rem(mid + e, mids)
            for d, peer in core_peers:
                back_core[c, e, d] = remote(
                    rows.at[pl.ds(place(lax.rem(core + d, cores), m, 0), fars), :, pl.ds(LANES + c * step, step)],
                    core_in.at[d - 1, pl.ds(m * fars, fars), :, pl.ds(c * step, step)],
                    rcore_s.at[c, e, d], rcore_r.at[c, e, d], peer)
        for e in range(1, mids):
            for d in range(1, cores):
                back_core[c, e, d].wait_recv()
        for d in back_order:
            send_mid(c, d)
    for c in range(PARTS):
        send_mid(c, 0)
    for c in range(PARTS):
        for d in range(1, cores):
            back_core[c, 0, d].wait_recv()
    for c in range(PARTS):
        cs = slice(c * step, (c + 1) * step)
        for d in back_order:
            peer = device(core, mid, other(d))
            far_out[d - 1, :, cs] = line_sum(c, d).astype(jnp.bfloat16)
            cols = pl.ds(c * step, step)
            back_far[c, d] = remote(far_out.at[d - 1, :, cols], far_in.at[d - 1, :, cols],
                                    rfar_s.at[c, d], rfar_r.at[c, d], peer)
    for c in range(PARTS):
        cs = slice(c * step, (c + 1) * step)
        far_own[:, cs] = line_sum(c, 0)
    for c in range(PARTS):
        cs = slice(c * step, (c + 1) * step)
        total = far_own[:, cs]
        for d in range(1, fars):
            back_far[c, d].wait_recv()
            total = total + far_in[d - 1, :, cs].astype(jnp.float32)
        for q in range(split):
            at = slice(q * part + c * step, q * part + (c + 1) * step)
            mixed = hid[:, at].astype(jnp.float32) + down_bias[:, at] + total[q * row_count:(q + 1) * row_count]
            out[:, at] = mixed.astype(out.dtype)
    for copies in [back_core.values(), back_mid.values(), back_far.values()]:
        for copy in copies:
            copy.wait_send()


def local(n_dev, hidden_in, active, ln_gain, ln_bias, up_weight, up_bias, down_weight, down_bias):
    fars, mids, cores = sizes(n_dev)
    width = hidden_in.shape[2]
    row_count = hidden_in.shape[0] * hidden_in.shape[1]
    split = PACK // row_count
    part = width // split
    units = up_weight.shape[1]
    plane = fars * mids
    vmem = pl.BlockSpec(memory_space=pltpu.VMEM)
    hbm = pl.BlockSpec(memory_space=pl.ANY)
    dma = pltpu.SemaphoreType.DMA
    bf16, f32 = jnp.bfloat16, jnp.float32
    out = pl.pallas_call(
        functools.partial(kernel, n_dev),
        out_shape=jax.ShapeDtypeStruct((row_count, width), bf16),
        in_specs=[vmem] * 6 + [hbm] * 2,
        out_specs=vmem,
        scratch_shapes=[
            pltpu.VMEM((n_dev, PACK, LANES + part), bf16),
            pltpu.VMEM((split, part, units), bf16),
            pltpu.VMEM((units, width), bf16),
            pltpu.VMEM((n_dev * PACK, units), f32),
            pltpu.VMEM((n_dev * PACK, split * units), bf16),
            pltpu.VMEM((max(cores - 1, 1), plane, PACK, part), bf16),
            pltpu.VMEM((max(mids - 1, 1), fars, PACK, part), bf16),
            pltpu.VMEM((max(mids - 1, 1), fars, PACK, part), bf16),
            pltpu.VMEM((max(fars - 1, 1), PACK, part), bf16),
            pltpu.VMEM((PACK, part), f32),
            pltpu.VMEM((max(fars - 1, 1), PACK, part), bf16),
            dma((PARTS,)), dma((PARTS, split)),
            dma((PARTS, fars)), dma((PARTS, fars)),
            dma((PARTS, fars, mids)), dma((PARTS, fars, mids)),
            dma((PARTS, mids, cores)), dma((PARTS, mids, cores)),
            dma((PARTS, mids, cores)), dma((PARTS, mids, cores)),
            dma((PARTS, fars, mids)), dma((PARTS, fars, mids)),
            dma((PARTS, fars)), dma((PARTS, fars)),
        ],
        compiler_params=pltpu.CompilerParams(
            collective_id=0, has_side_effects=True, vmem_limit_bytes=60 * 1024 * 1024),
    )(
        hidden_in.reshape(row_count, width), active.reshape(row_count, -1),
        ln_gain.reshape(1, -1), ln_bias.reshape(1, -1), up_bias.reshape(1, -1), down_bias.reshape(1, -1),
        up_weight.reshape(split, part, units), down_weight,
    )
    return out.reshape(hidden_in.shape)


def solution(mesh):
    in_specs = (
        P(None, ("groups", "tensor"), None),
        P(None, ("groups", "tensor"), None),
        P(),
        P(),
        P(None, "tensor"),
        P("tensor"),
        P("tensor", None),
        P(),
    )
    out_specs = P(None, ("groups", "tensor"), None)
    return jax.shard_map(
        functools.partial(local, mesh.shape["tensor"]), mesh=mesh, in_specs=in_specs, out_specs=out_specs,
        check_vma=False)
```
